32 devices in a mesh: groups: 2 (over y), mem: 4 (over x, core), tp: 4 (over z).
Axes of the slice: x: 2, y: 2, z: 4, core: 2. Of those that a mesh axis runs over, the one named last changes fastest.
Arguments:
- questions: bfloat16 [16, 32, 4096], P(('groups', 'mem'), None, 'tp'), parts along dimension 0
- memory: bfloat16 [512, 64, 4096], P(('groups', 'mem'), None, 'tp'), parts along dimension 0
- pass_ids: int32 [16, 10], P('groups'), parts along dimension 0, may hold values from 0 to 255, as said below
- pass_map: int32 [512], P('groups'), parts along dimension 0, may hold values from 0 to 255, as said below
- norm_gain: bfloat16 [1, 4096], P(None, 'tp'), may hold values from 0.25 to 1.75
- w_query: bfloat16 [4096, 4096], P(None, 'tp')
- w_key: bfloat16 [4096, 4096], P(None, 'tp')
- w_value: bfloat16 [4096, 4096], P(None, 'tp'), may hold values from -0.375 to 0.375
- w_out: bfloat16 [4096, 4096], P('tp'), may hold values from -0.1875 to 0.1875
Outputs:
- mixed: bfloat16 [16, 10, 96, 4096], P(('groups', 'mem'), None, None, 'tp'), parts along dimension 0
The draws below stay inside these ranges and needn't reach their ends.
There are 2 independent parts, one for each index of `groups`. The reference program is written for one: setup_inputs(seed, part) draws one part's arguments, and reference() takes and returns one part's arrays. A program takes and returns all parts, laid end to end along the dimension named above; an argument that names none is the same for every part. Nothing has to cross between parts.
Inputs may be any that keep to these rules, and one draw needn't show every extreme that they name: `pass_ids`: each question lists 10 different passages; of the 20 passages listed by the questions of one index of mem, at most 10 are stored on any one index of mem (storage rows k * 64 to (k + 1) * 64 - 1 for index k), and exactly 10 on some index. Passage p is stored at row pass_map[p] of memory; each row holds one passage.
All inputs are finite; a program needn't handle non-finite values.
Results may differ from the reference program's by a relative error of at most 0.0048.
Values may be sent and summed in bfloat16 or wider, within the bound.
A program may use at most 192 MiB of HBM per device.

```python
import math
import jax
import jax.numpy as jnp
from jax import lax

D = 4096
HEADS = 64
HDIM = 64
QDEV = 2
SLOTS = 64
NPASS = 10
QLEN = 32
PLEN = 64
QUESTIONS = 8
PASSAGES = 256
CAP = 10
N_MEM = 4


def apply_scales(key, base, col_top, row_top):
    feat_width = base.shape[-1]
    key_rows = jax.random.fold_in(key, 0)
    columns = 0.3 * col_top ** (jnp.arange(feat_width, dtype=jnp.float32) / (feat_width - 1))
    row_shape = base.shape[:-1] + (1,)
    row_scale = 0.3 * jnp.exp(jax.random.uniform(key_rows, row_shape, jnp.float32) * math.log(row_top))
    return base * columns * row_scale


def draw_questions(key, part):
    key = jax.random.fold_in(key, 11)
    key_base, key_scale = jax.random.split(key)
    shape = (QUESTIONS, QLEN, D)
    base = jax.random.normal(key_base, shape, jnp.float32)
    field = apply_scales(key_scale, base, 10.0, 10.0)
    return field.astype(jnp.bfloat16)


def draw_memory(key, part):
    key = jax.random.fold_in(key, 13)
    key_base, key_scale = jax.random.split(key)
    shape = (PASSAGES, PLEN, D)
    base = jax.random.normal(key_base, shape, jnp.float32)
    field = apply_scales(key_scale, base, 10.0, 10.0)
    return field.astype(jnp.bfloat16)


def stored_order(key):
    return jax.random.permutation(jax.random.fold_in(key, 71), PASSAGES).astype(jnp.int32)


def draw_pass_map(key, part):
    return stored_order(key)


def draw_pass_ids(key, part):
    order = stored_order(key)
    inverse = jnp.zeros((PASSAGES,), jnp.int32).at[order].set(jnp.arange(PASSAGES, dtype=jnp.int32))
    key = jax.random.fold_in(key, 3)
    per_reader = QDEV * NPASS
    spare_count = per_reader - CAP

    def one_reader(reader_key):
        key_first, key_spare, key_order, key_rows = jax.random.split(reader_key, 4)
        first = jax.random.randint(key_first, (), 0, N_MEM).astype(jnp.int32)
        spare = jax.random.permutation(key_spare, (N_MEM - 1) * CAP).astype(jnp.int32)[:spare_count] // CAP
        owners = jnp.concatenate([jnp.full((CAP,), first, jnp.int32), (first + 1 + spare) % N_MEM])
        owners = owners[jax.random.permutation(key_order, per_reader).astype(jnp.int32)]
        position = jnp.arange(per_reader, dtype=jnp.int32)
        earlier = position[:, None] > position[None, :]
        same = owners[:, None] == owners[None, :]
        rank = jnp.sum((same & earlier).astype(jnp.int32), axis=1)
        row_keys = jax.random.split(key_rows, N_MEM)
        shuffles = jax.vmap(lambda one_key: jax.random.permutation(one_key, SLOTS).astype(jnp.int32))(row_keys)
        rows = owners * SLOTS + shuffles[owners, rank]
        return inverse[rows]
    reader_keys = jax.random.split(key, N_MEM)
    listed = jax.vmap(one_reader)(reader_keys)
    return listed.reshape(QUESTIONS, NPASS).astype(jnp.int32)


def query_matrix(key):
    return jax.random.normal(jax.random.fold_in(key, 5), (D, D), jnp.float32) * (D * HDIM) ** (-0.5)


def draw_w_query(key, part):
    return query_matrix(key).astype(jnp.bfloat16)


def draw_w_key(key, part):
    key = jax.random.fold_in(key, 19)
    noise = jax.random.normal(key, (D, D), jnp.float32) * (D * HDIM) ** (-0.5)
    matrix = noise
    return matrix.astype(jnp.bfloat16)


def level_of(rng, dims, cuts, smallest, largest):
    factor_of = 1.0
    for dim, shards_of in cuts:
        heights = jax.random.uniform(jax.random.fold_in(jax.random.fold_in(rng, 6), dim), (shards_of,), jnp.float32, smallest / len(cuts), largest / len(cuts))
        factor_of = factor_of * jnp.repeat(jnp.exp(heights), dims[dim] // shards_of).reshape((-1,) + (1,) * (len(dims) - 1 - dim))
    return factor_of


def scatter_about(stream_key, shape, scale, limit, cuts=(), kind=jnp.bfloat16):
    result = jax.random.normal(stream_key, shape, jnp.float32) * scale
    if len(cuts) > 0:
        result = level_of(stream_key, shape, cuts, -0.22, 0.18) * result
    return jnp.clip(result, min=-limit, max=limit).astype(kind)


def setup_inputs(seed: int = 0, part: int = 0) -> dict:
    key_of = jax.random.split(jax.random.key(seed), 10)
    part_splits = jax.random.split(jax.random.fold_in(key_of[9], part), 10)
    questions = draw_questions(jax.random.fold_in(jax.random.fold_in(key_of[9], part), 71), part)
    memory = draw_memory(jax.random.fold_in(jax.random.fold_in(key_of[9], part), 71), part)
    pass_ids = draw_pass_ids(jax.random.fold_in(jax.random.fold_in(key_of[9], part), 71), part)
    pass_map = draw_pass_map(jax.random.fold_in(jax.random.fold_in(key_of[9], part), 71), part)
    norm_gain = jnp.clip(1.0 + 0.15 * jax.random.normal(key_of[4], (1, D), jnp.float32), 0.25, 1.75).astype(jnp.bfloat16)
    w_query = draw_w_query(jax.random.fold_in(key_of[9], 71), part)
    w_key = draw_w_key(jax.random.fold_in(key_of[9], 71), part)
    w_value = scatter_about(key_of[7], (D, D), (D // 16) ** -0.5, 0.375, ((1, 4),))
    w_out = scatter_about(key_of[8], (D, D), (D // 4) ** -0.5, 0.1875, ((0, 4),))
    return {"questions": questions, "memory": memory, "pass_ids": pass_ids, "pass_map": pass_map, "norm_gain": norm_gain, "w_query": w_query, "w_key": w_key, "w_value": w_value, "w_out": w_out}


def normalize(rows, gain):
    wide = rows.astype(jnp.float32)
    factor = lax.rsqrt(lax.optimization_barrier(jnp.mean(wide * wide, axis=-1, keepdims=True)) + 1e-06)
    return (wide * factor * gain.astype(jnp.float32)).astype(jnp.bfloat16)

def project(rows, matrix):
    flat = rows.reshape(-1, D)
    return jnp.dot(flat, matrix, preferred_element_type=jnp.float32).astype(jnp.bfloat16)

def pair_rows(ques_part, pass_part, last_shape):
    ques_wide = jnp.broadcast_to(ques_part.reshape((QUESTIONS, 1, QLEN) + last_shape), (QUESTIONS, NPASS, QLEN) + last_shape)
    pass_wide = pass_part.reshape((QUESTIONS, NPASS, PLEN) + last_shape)
    return jnp.concatenate([ques_wide, pass_wide], axis=2)

def reference(questions, memory, pass_ids, pass_map, norm_gain, w_query, w_key, w_value, w_out):
    location = jnp.take(pass_map, pass_ids.reshape(-1), axis=0)
    fetched = jnp.take(memory, location, axis=0).reshape(QUESTIONS, NPASS, PLEN, D)
    gain = norm_gain[0]
    ques_norm = normalize(questions, gain)
    pass_norm = normalize(fetched, gain)
    head_shape = (HEADS, HDIM)
    queries = pair_rows(project(ques_norm, w_query), project(pass_norm, w_query), head_shape)
    keys_all = pair_rows(project(ques_norm, w_key), project(pass_norm, w_key), head_shape)
    values_all = pair_rows(project(ques_norm, w_value), project(pass_norm, w_value), head_shape)
    inputs = pair_rows(questions, fetched, (D,))

    def one_question(operands):
        q_one, k_one, v_one, x_one = operands
        scores = jnp.einsum('nqhe,nkhe->nhqk', q_one.astype(jnp.float32), k_one.astype(jnp.float32))
        scores = scores - lax.optimization_barrier(jnp.max(scores, axis=-1, keepdims=True))
        expd = jnp.exp(scores)
        probs = (expd / lax.optimization_barrier(jnp.sum(expd, axis=-1, keepdims=True))).astype(jnp.bfloat16)
        context = jnp.einsum('nhqk,nkhe->nqhe', probs.astype(jnp.float32), v_one.astype(jnp.float32))
        context = context.astype(jnp.bfloat16).reshape(NPASS * (QLEN + PLEN), D)
        branch = jnp.dot(context, w_out, preferred_element_type=jnp.float32)
        summed = x_one.reshape(NPASS * (QLEN + PLEN), D).astype(jnp.float32) + branch
        return summed.astype(jnp.bfloat16).reshape(NPASS, QLEN + PLEN, D)
    return lax.map(one_question, (queries, keys_all, values_all, inputs))
```

```python
import jax
import jax.numpy as jnp
from jax import lax
from jax.experimental import pallas as pl
from jax.experimental.pallas import tpu as pltpu
from jax.sharding import PartitionSpec as P

HDIM = 64
PLEN = 64
GATHER = "native"
REDUCE = "native"
CHUNKS = 5
RING_MAX = 8


def line_gather(rows, axis):
    n = lax.axis_size(axis)
    if GATHER == "native" or n > RING_MAX:
        return lax.all_gather(rows, axis, axis=1, tiled=True)
    width = rows.shape[1]
    from_left, from_right = [], []
    right, left = rows, rows
    for step in range(1, n):
        right = lax.ppermute(right, axis, [(i, i + 1) for i in range(step - 1, n - 1)])
        left = lax.ppermute(left, axis, [(i, i - 1) for i in range(1, n - step + 1)])
        from_left.append(right)
        from_right.append(left)
    strip = jnp.concatenate(from_left[::-1] + [rows] + from_right, axis=1)
    me = lax.axis_index(axis)
    return lax.dynamic_slice_in_dim(strip, (n - 1 - me) * width, n * width, 1)


def line_reduce(terms, axis):
    n = lax.axis_size(axis)
    if REDUCE == "native" or n > RING_MAX:
        return lax.psum_scatter(terms, axis, scatter_dimension=1, tiled=True).astype(jnp.float32)
    width = terms.shape[1] // n
    me = lax.axis_index(axis)

    def block(index):
        start = jnp.clip(index, 0, n - 1) * width
        return lax.dynamic_slice_in_dim(terms, start, width, 1)

    right = left = None
    for step in range(1, n):
        reach = n - step
        out_right, out_left = block(me + reach), block(me - reach)
        if step > 1:
            out_right = (out_right.astype(jnp.float32) + right.astype(jnp.float32)).astype(jnp.bfloat16)
            out_left = (out_left.astype(jnp.float32) + left.astype(jnp.float32)).astype(jnp.bfloat16)
        right = lax.ppermute(out_right, axis, [(i, i + 1) for i in range(step)])
        left = lax.ppermute(out_left, axis, [(i, i - 1) for i in range(n - step, n)])
    return block(me).astype(jnp.float32) + right.astype(jnp.float32) + left.astype(jnp.float32)


def attend_kernel(ques_ref, qq, kq, vq, qp, kp, vp, out):
    del ques_ref
    total = qq.shape[0] + qp.shape[0]
    first = lax.broadcasted_iota(jnp.int32, (total, 2 * HDIM), 1) < HDIM
    zero = jnp.zeros((total, 2 * HDIM), jnp.bfloat16)
    for j in range(qq.shape[1] // (2 * HDIM)):
        cols = slice(j * 2 * HDIM, (j + 1) * 2 * HDIM)
        q = jnp.concatenate([qq[:, cols], qp[:, cols]], axis=0)
        k = jnp.concatenate([kq[:, cols], kp[:, cols]], axis=0)
        v = jnp.concatenate([vq[:, cols], vp[:, cols]], axis=0)
        both = jnp.concatenate([jnp.where(first, q, zero), jnp.where(first, zero, q)], axis=0)
        scores = lax.dot_general(both, k, (((1,), (1,)), ((), ())), preferred_element_type=jnp.float32)
        expd = jnp.exp(scores - jnp.max(scores, axis=-1, keepdims=True))
        probs = (expd / jnp.sum(expd, axis=-1, keepdims=True)).astype(jnp.bfloat16)
        ctx = jnp.dot(probs, v, preferred_element_type=jnp.float32)
        out[:, cols] = jnp.where(first, ctx[:total], ctx[total:]).astype(jnp.bfloat16)


def attend(question_of, ques, passages, qlen):
    count = question_of.shape[0]
    width = ques[0].shape[1]
    seq = qlen + PLEN
    ques_spec = pl.BlockSpec((qlen, width), lambda i, q: (q[i], 0))
    pass_spec = pl.BlockSpec((PLEN, width), lambda i, q: (i, 0))
    return pl.pallas_call(
        attend_kernel,
        grid_spec=pltpu.PrefetchScalarGridSpec(
            num_scalar_prefetch=1,
            grid=(count,),
            in_specs=[ques_spec] * 3 + [pass_spec] * 3,
            out_specs=pl.BlockSpec((seq, width), lambda i, q: (i, 0)),
        ),
        out_shape=jax.ShapeDtypeStruct((count * seq, width), jnp.bfloat16),
        cost_estimate=pl.CostEstimate(
            flops=8 * count * seq * seq * width,
            bytes_accessed=8 * count * seq * width,
            transcendentals=count * seq * seq * width // HDIM,
        ),
    )(question_of, *ques, *passages)


def normalize(rows, gain):
    wide = rows.astype(jnp.float32)
    factor = lax.rsqrt(jnp.mean(wide * wide, axis=1, keepdims=True) + 1e-06)
    return (wide * factor * gain.astype(jnp.float32)).astype(jnp.bfloat16)


def project(rows, weights):
    return [jnp.dot(rows, w, preferred_element_type=jnp.float32).astype(jnp.bfloat16) for w in weights]


def local(questions, memory, pass_ids, pass_map, norm_gain, w_query, w_key, w_value, w_out):
    readers = lax.axis_size("mem")
    own_index = lax.axis_index("mem")
    q_count, qlen, feat_width = questions.shape
    npass = pass_ids.shape[1]
    slot_count = memory.shape[0]
    stored = pass_map.shape[0]
    per_reader = q_count * npass
    capacity = min(per_reader, 2 * -(-per_reader // readers))
    weights = (w_query, w_key, w_value)

    matches = pass_ids[:, :, None] == jnp.arange(stored, dtype=jnp.int32)[None, None, :]
    location = jnp.sum(jnp.where(matches, pass_map[None, None, :], 0), axis=2).reshape(readers, per_reader)
    owners = location // slot_count
    position = jnp.arange(per_reader, dtype=jnp.int32)
    earlier = position[:, None] > position[None, :]
    mine = owners == own_index
    rank_mine = jnp.sum((mine[:, None, :] & earlier[None, :, :]).astype(jnp.int32), axis=2)
    slot_ids = jnp.arange(capacity, dtype=jnp.int32)
    pick = mine[:, None, :] & (rank_mine[:, None, :] == slot_ids[None, :, None])
    slot_rows = jnp.sum(jnp.where(pick, (location % slot_count)[:, None, :], 0), axis=2)

    sources = lax.dynamic_index_in_dim(owners, own_index, 0, keepdims=False)
    same_source = sources[:, None] == sources[None, :]
    rank_here = jnp.sum((same_source & earlier).astype(jnp.int32), axis=1)
    order_key = rank_here * per_reader + position
    place = jnp.sum((order_key[None, :] < order_key[:, None]).astype(jnp.int32), axis=1)
    at_place = place[None, :] == position[:, None]

    def in_order(values):
        return jnp.sum(jnp.where(at_place, values[None, :], 0), axis=1)

    listed = in_order(position)
    source_of, rank_of = in_order(sources), in_order(rank_here)
    question_of = listed // npass

    chunks = CHUNKS if per_reader % CHUNKS == 0 and capacity % CHUNKS == 0 else 1
    ranks, count = capacity // chunks, per_reader // chunks
    slot_of = ((rank_of // ranks) * readers + source_of) * ranks + rank_of % ranks

    question_rows = questions.reshape(q_count * qlen, feat_width)
    head_rows = line_gather(jnp.concatenate([question_rows, norm_gain], axis=0), "tp")
    gain = head_rows[q_count * qlen :]
    ques_qkv = project(normalize(head_rows[: q_count * qlen], gain), weights)

    incoming, finished = [], []
    for c in range(chunks):
        rows = slot_rows[:, c * ranks : (c + 1) * ranks]
        picked = jnp.take(memory, rows.reshape(-1), axis=0).reshape(readers, ranks, PLEN, feat_width)
        arrived = lax.all_to_all(picked, "mem", split_axis=0, concat_axis=0, tiled=True)
        incoming.append(arrived.reshape(readers * ranks, PLEN, feat_width))
        part = slice(c * count, (c + 1) * count)
        pool = jnp.concatenate(incoming, axis=0) if c else incoming[0]
        fetched = jnp.take(pool, slot_of[part], axis=0)
        full = line_gather(fetched.reshape(count * PLEN, feat_width), "tp")
        pass_qkv = project(normalize(full, gain), weights)
        context = attend(question_of[part], ques_qkv, pass_qkv, qlen)
        terms = jnp.dot(context, w_out, preferred_element_type=jnp.float32).astype(jnp.bfloat16)
        branch = line_reduce(terms, "tp").reshape(count, qlen + PLEN, feat_width)
        residual = jnp.concatenate([jnp.take(questions, question_of[part], axis=0), fetched], axis=1)
        finished.append((residual.astype(jnp.float32) + branch).astype(jnp.bfloat16))
    mixed = jnp.take(jnp.concatenate(finished, axis=0), place, axis=0)
    return mixed.reshape(q_count, npass, qlen + PLEN, feat_width)


def solution(mesh):
    in_specs = (
        P(("groups", "mem"), None, "tp"),
        P(("groups", "mem"), None, "tp"),
        P("groups", None),
        P("groups"),
        P(None, "tp"),
        P(None, "tp"),
        P(None, "tp"),
        P(None, "tp"),
        P("tp", None),
    )
    out_specs = P(("groups", "mem"), None, None, "tp")
    return jax.shard_map(local, mesh=mesh, in_specs=in_specs, out_specs=out_specs, check_vma=False)
```

```python
import jax
import jax.numpy as jnp
from jax import lax
from jax.experimental import pallas as pl
from jax.experimental.pallas import tpu as pltpu
from jax.sharding import PartitionSpec as P

HDIM = 64
PLEN = 64
GATHER = "native"
REDUCE = "native"
TENTHS = (3, 7)
RING_MAX = 8


def attend_kernel(ques_ref, qq, kq, vq, qp, kp, vp, out):
    del ques_ref
    total = qq.shape[0] + qp.shape[0]
    first = lax.broadcasted_iota(jnp.int32, (total, 2 * HDIM), 1) < HDIM
    zero = jnp.zeros((total, 2 * HDIM), jnp.bfloat16)
    for j in range(qq.shape[1] // (2 * HDIM)):
        cols = slice(j * 2 * HDIM, (j + 1) * 2 * HDIM)
        q = jnp.concatenate([qq[:, cols], qp[:, cols]], axis=0)
        k = jnp.concatenate([kq[:, cols], kp[:, cols]], axis=0)
        v = jnp.concatenate([vq[:, cols], vp[:, cols]], axis=0)
        both = jnp.concatenate([jnp.where(first, q, zero), jnp.where(first, zero, q)], axis=0)
        scores = lax.dot_general(both, k, (((1,), (1,)), ((), ())), preferred_element_type=jnp.float32)
        expd = jnp.exp(scores - jnp.max(scores, axis=-1, keepdims=True))
        probs = (expd / jnp.sum(expd, axis=-1, keepdims=True)).astype(jnp.bfloat16)
        ctx = jnp.dot(probs, v, preferred_element_type=jnp.float32)
        out[:, cols] = jnp.where(first, ctx[:total], ctx[total:]).astype(jnp.bfloat16)


def attend(question_of, ques, passages, qlen):
    count = question_of.shape[0]
    width = ques[0].shape[1]
    seq = qlen + PLEN
    ques_spec = pl.BlockSpec((qlen, width), lambda i, q: (q[i], 0))
    pass_spec = pl.BlockSpec((PLEN, width), lambda i, q: (i, 0))
    return pl.pallas_call(
        attend_kernel,
        grid_spec=pltpu.PrefetchScalarGridSpec(
            num_scalar_prefetch=1,
            grid=(count,),
            in_specs=[ques_spec] * 3 + [pass_spec] * 3,
            out_specs=pl.BlockSpec((seq, width), lambda i, q: (i, 0)),
        ),
        out_shape=jax.ShapeDtypeStruct((count * seq, width), jnp.bfloat16),
        cost_estimate=pl.CostEstimate(
            flops=8 * count * seq * seq * width,
            bytes_accessed=8 * count * seq * width,
            transcendentals=count * seq * seq * width // HDIM,
        ),
    )(question_of, *ques, *passages)


def normalize(rows, gain):
    wide = rows.astype(jnp.float32)
    factor = lax.rsqrt(jnp.mean(wide * wide, axis=1, keepdims=True) + 1e-06)
    return (wide * factor * gain.astype(jnp.float32)).astype(jnp.bfloat16)


def project(rows, weights):
    return [jnp.dot(rows, w, preferred_element_type=jnp.float32).astype(jnp.bfloat16) for w in weights]


def local(questions, memory, pass_ids, pass_map, norm_gain, w_query, w_key, w_value, w_out):
    readers = lax.axis_size("mem")
    own_index = lax.axis_index("mem")
    q_count, qlen, feat_width = questions.shape
    npass = pass_ids.shape[1]
    slot_count = memory.shape[0]
    stored = pass_map.shape[0]
    per_reader = q_count * npass
    capacity = min(per_reader, 2 * -(-per_reader // readers))
    weights = (w_query, w_key, w_value)

    matches = pass_ids[:, :, None] == jnp.arange(stored, dtype=jnp.int32)[None, None, :]
    location = jnp.sum(jnp.where(matches, pass_map[None, None, :], 0), axis=2).reshape(readers, per_reader)
    owners = location // slot_count
    position = jnp.arange(per_reader, dtype=jnp.int32)
    earlier = position[:, None] > position[None, :]
    mine = owners == own_index
    rank_mine = jnp.sum((mine[:, None, :] & earlier[None, :, :]).astype(jnp.int32), axis=2)
    slot_ids = jnp.arange(capacity, dtype=jnp.int32)
    pick = mine[:, None, :] & (rank_mine[:, None, :] == slot_ids[None, :, None])
    slot_rows = jnp.sum(jnp.where(pick, (location % slot_count)[:, None, :], 0), axis=2)

    sources = lax.dynamic_index_in_dim(owners, own_index, 0, keepdims=False)
    same_source = sources[:, None] == sources[None, :]
    rank_here = jnp.sum((same_source & earlier).astype(jnp.int32), axis=1)
    order_key = rank_here * per_reader + position
    place = jnp.sum((order_key[None, :] < order_key[:, None]).astype(jnp.int32), axis=1)
    at_place = place[None, :] == position[:, None]

    def in_order(values):
        return jnp.sum(jnp.where(at_place, values[None, :], 0), axis=1)

    listed = in_order(position)
    source_of, rank_of = in_order(sources), in_order(rank_here)
    question_of = listed // npass

    split = TENTHS if sum(TENTHS) == capacity and per_reader % capacity == 0 else (capacity,)
    starts = [sum(split[:c]) for c in range(len(split))]
    slot_of = jnp.zeros_like(rank_of)
    for start, ranks in zip(starts, split):
        slot_of = jnp.where(rank_of >= start, start * readers + source_of * ranks + rank_of - start, slot_of)

    question_rows = questions.reshape(q_count * qlen, feat_width)
    head_rows = lax.all_gather(jnp.concatenate([question_rows, norm_gain], axis=0), "tp", axis=1, tiled=True)
    gain = head_rows[q_count * qlen :]
    ques_qkv = project(normalize(head_rows[: q_count * qlen], gain), weights)

    incoming, finished = [], []
    for c, (start, ranks) in enumerate(zip(starts, split)):
        count = ranks * per_reader // capacity
        rows = slot_rows[:, start : start + ranks]
        picked = jnp.take(memory, rows.reshape(-1), axis=0, mode="clip").reshape(readers, ranks, PLEN, feat_width)
        arrived = lax.all_to_all(picked, "mem", split_axis=0, concat_axis=0, tiled=True)
        incoming.append(arrived.reshape(readers * ranks, PLEN, feat_width))
        part = slice(start * per_reader // capacity, (start + ranks) * per_reader // capacity)
        pool = jnp.concatenate(incoming, axis=0) if c else incoming[0]
        fetched = jnp.take(pool, slot_of[part], axis=0, mode="clip")
        full = lax.all_gather(fetched.reshape(count * PLEN, feat_width), "tp", axis=1, tiled=True)
        pass_qkv = project(normalize(full, gain), weights)
        context = attend(question_of[part], ques_qkv, pass_qkv, qlen)
        terms = jnp.dot(context, w_out, preferred_element_type=jnp.float32).astype(jnp.bfloat16)
        branch = lax.psum_scatter(terms, "tp", scatter_dimension=1, tiled=True).reshape(count, qlen + PLEN, feat_width)
        residual = jnp.concatenate([jnp.take(questions, question_of[part], axis=0, mode="clip"), fetched], axis=1)
        finished.append((residual.astype(jnp.float32) + branch.astype(jnp.float32)).astype(jnp.bfloat16))
    mixed = jnp.take(jnp.concatenate(finished, axis=0), place, axis=0, mode="clip")
    return mixed.reshape(q_count, npass, qlen + PLEN, feat_width)


def solution(mesh):
    in_specs = (
        P(("groups", "mem"), None, "tp"),
        P(("groups", "mem"), None, "tp"),
        P("groups", None),
        P("groups"),
        P(None, "tp"),
        P(None, "tp"),
        P(None, "tp"),
        P(None, "tp"),
        P("tp", None),
    )
    out_specs = P(("groups", "mem"), None, None, "tp")
    return jax.shard_map(local, mesh=mesh, in_specs=in_specs, out_specs=out_specs, check_vma=False)
```
